1024 devices in a mesh: node: 64 (over z, y), local: 16 (over x, core).
Axes of the slice: x: 8, y: 8, z: 8, core: 2. Of those that a mesh axis runs over, the one named last changes fastest.
Arguments:
- tokens: bfloat16 [6144, 7168], P('node', 'local'), may hold values from -6 to 6
- expert_ids: int32 [6144, 8], P('node'), may hold values from 0 to 15, all different within a row; in each aligned block of 96 rows (0 to 95, 96 to 191, ...) at most 72 rows name the same one
- route_weight: float32 [6144, 8], P('node'), may hold values from 0.05 to 0.4
- pool_offset: int32 [64, 16], P('node'), may hold values from 0 to 3
- gate_up: bfloat16 [64, 7168, 2048], P('node', 'local'), may hold values from -0.0625 to 0.0625
- down_proj: bfloat16 [64, 1024, 7168], P('node', None, 'local'), may hold values from -0.1875 to 0.1875
- shared_gate_up: bfloat16 [7168, 2048], P('local'), may hold values from -0.0625 to 0.0625
- shared_down: bfloat16 [1024, 7168], P(None, 'local'), may hold values from -0.1875 to 0.1875
Outputs:
- mixed: bfloat16 [6144, 7168], P('node', 'local')
The draws below stay inside these ranges and needn't reach their ends.
Inputs may be any that keep to these rules, and one draw needn't show every extreme that they name: `expert_ids`: each row names 8 different experts; within the 96 rows of one node no expert is named more than 72 times, and in some node one expert is named exactly 72 times.
All inputs are finite; a program needn't handle non-finite values.
Results may differ from the reference program's by a relative error of at most 0.03.
Values may be sent and summed in bfloat16 or wider, within the bound.
A program may use at most 64 MiB of HBM per device.

```python
import math
import jax
import jax.numpy as jnp
import numpy as np
from jax import lax

D = 7168
FF = 1024
SH = 1024
TOK_NODE = 96
POOLS = 4
EXPERTS = 16
TOPK = 8
MOST = 72
CAP = 18
TOKENS = 6144
N_NODE = 64
N_LOCAL = 16


def set_ends(array, rng, least, largest):
    spot = [jax.random.randint(jax.random.fold_in(rng, axis), (), 0, length) for axis, length in enumerate(array.shape)]
    main_axis = array.shape.index(max(array.shape))
    neighbour = spot[:main_axis] + [(spot[main_axis] + 1) % array.shape[main_axis]] + spot[main_axis + 1:]
    return array.at[tuple(spot)].set(least).at[tuple(neighbour)].set(largest)


def block_levels(own_key, dims, split, smallest, high):
    factor_of = 1.0
    for dim, parts in split:
        heights = jax.random.uniform(jax.random.fold_in(jax.random.fold_in(own_key, 6), dim), (parts,), jnp.float32, smallest / len(split), high / len(split))
        factor_of = factor_of * jnp.repeat(jnp.exp(heights), dims[dim] // parts).reshape((-1,) + (1,) * (len(dims) - 1 - dim))
    return factor_of


def routed_block(rng, own, number, rows, count, top, reach, lean):
    order = jax.random.permutation(rng, count)
    heavy_load, usual = shares(count, rows * top, reach, lean, True), shares(count, rows * top, reach, lean, False)
    places = jnp.arange(count)

    def named(tallies, offset_by):
        used = int((tallies > 0).sum())
        fixed = max(1, used // 4)
        passed = fixed + (places - fixed + offset_by * (used - fixed)) % max(1, count - fixed)
        return jnp.zeros((count,), jnp.int32).at[order[jnp.where(places < fixed, places, passed)]].set(jnp.asarray(tallies, jnp.int32))

    tallies = jnp.where(number % 4 == 0, named(heavy_load, number // 4), named(usual, number - number // 4 - 1))
    mixed = jax.random.permutation(jax.random.fold_in(own, 3), count)
    giver, sink = mixed[0:count // 2 * 2:2], mixed[1:count // 2 * 2:2]
    slack = jnp.minimum(tallies[giver] - 1, reach - tallies[sink]) // 2
    slack = jnp.where((giver == order[0]) | (sink == order[0]) | (tallies[sink] == 0), 0, jnp.maximum(slack, 0))
    passed = jax.random.randint(jax.random.fold_in(own, 4), (count // 2,), 0, 1 << 20) % (slack + 1)
    tallies = tallies.at[giver].add(-passed).at[sink].add(passed)
    members = jnp.searchsorted(jnp.cumsum(tallies), jnp.arange(rows * top), side="right").astype(jnp.int32)
    grid = members.reshape(top, rows).T
    grid = grid[jax.random.permutation(jax.random.fold_in(own, 1), rows)]
    offset_by = jax.random.randint(jax.random.fold_in(own, 2), (rows, 1), 0, top)
    return jnp.take_along_axis(grid, (jnp.arange(top)[None, :] + offset_by) % top, axis=1)


def shares(count, total, limit, skew, full):
    loads = [(1 << 20) // math.isqrt(standing ** skew) + 1 for standing in range(1, count + 1)]
    largest = limit if full else min(limit, max(-(-total // count), total * loads[0] // sum(loads)))
    least = 1 if total - largest >= count - 1 else 0
    counts, spare = [largest] + [least] * (count - 1), total - largest - least * (count - 1)
    while spare > 0:
        free = [i for i in range(1, count) if counts[i] < largest] or [i for i in range(1, count) if counts[i] < limit]
        whole, budget = sum([loads[i] for i in free]), spare
        for i in free:
            more = min(limit - counts[i], max(1, budget * loads[i] // whole), spare)
            counts[i] = counts[i] + more
            spare = spare - more
    return np.array(counts)


def bell_draw(key, extent, spread, reach, shards=(), kind=jnp.bfloat16):
    level = block_levels(key, extent, shards, -0.22, 0.18) if shards else 1.0
    result = jax.random.normal(key, extent, jnp.float32) * spread * level
    return jnp.minimum(jnp.maximum(result, -reach), reach).astype(kind)


def setup_inputs(seed: int = 0) -> dict:
    keys = jax.random.split(jax.random.key(seed), 9)
    tokens = bell_draw(keys[0], (TOKENS, D), 1.0, 6.0, ((0, 64), (1, 16)))
    expert_ids_keys = jax.random.split(jax.random.fold_in(keys[1], 1), TOKENS // TOK_NODE)
    expert_ids_turns = jax.random.permutation(jax.random.fold_in(keys[1], 3), TOKENS // TOK_NODE)
    expert_ids = jax.vmap(lambda own, number: routed_block(jax.random.fold_in(keys[1], 2), own, number, TOK_NODE, EXPERTS, TOPK, MOST, 1))(expert_ids_keys, expert_ids_turns).reshape((TOKENS, TOPK))
    route_weight = jnp.clip(0.05 + 0.35 * jax.random.uniform(keys[2], (TOKENS, TOPK), jnp.float32) ** block_levels(keys[2], (TOKENS, TOPK), ((0, 64),), -0.2, 0.2), 0.05, 0.4)
    pool_offset = set_ends(jax.random.randint(keys[3], (N_NODE, EXPERTS), 0, POOLS), jax.random.fold_in(keys[3], 1), 0, POOLS - 1).astype(jnp.int32)
    gate_up = bell_draw(keys[4], (N_NODE, D, 2 * FF), D ** -0.5, 0.0625, ((0, 64), (1, 16)))
    down_proj = bell_draw(keys[5], (N_NODE, FF, D), FF ** -0.5, 0.1875, ((0, 64), (2, 16)))
    shared_gate_up = bell_draw(keys[6], (D, 2 * SH), D ** -0.5, 0.0625, ((0, 16),))
    shared_down = bell_draw(keys[7], (SH, D), SH ** -0.5, 0.1875, ((1, 16),))
    return dict(tokens=tokens, expert_ids=expert_ids, route_weight=route_weight, pool_offset=pool_offset, gate_up=gate_up, down_proj=down_proj, shared_gate_up=shared_gate_up, shared_down=shared_down)


def blocked_hidden(rows, weights, width_local, units):
    count = rows.shape[0]
    blocks = rows.reshape(count, N_LOCAL, width_local).astype(jnp.float32)
    wide = weights.reshape(N_LOCAL, width_local, 2 * units).astype(jnp.float32)
    partial_value = jnp.einsum("sjd,jdf->sjf", blocks, wide)
    rounded = lax.optimization_barrier(partial_value.astype(jnp.bfloat16))
    total = rounded.astype(jnp.float32).sum(axis=1)
    grouped = total.reshape(count, N_LOCAL, 2, units // N_LOCAL)
    gate = grouped[:, :, 0, :].reshape(count, units)
    upper = grouped[:, :, 1, :].reshape(count, units)
    return (jax.nn.silu(gate) * upper).astype(jnp.bfloat16)


def reference(tokens, expert_ids, route_weight, pool_offset, gate_up, down_proj, shared_gate_up, shared_down):
    token_count = tokens.shape[0]
    width_local = D // N_LOCAL
    home_node = jnp.arange(token_count, dtype=jnp.int32) // TOK_NODE
    matches = (expert_ids[:, :, None] == jnp.arange(EXPERTS, dtype=jnp.int32)).astype(jnp.int32)
    per_token = matches.sum(axis=1).reshape(N_NODE, TOK_NODE, EXPERTS)
    before = (jnp.cumsum(per_token, axis=1) - per_token).reshape(token_count, EXPERTS)
    arrival_rank = jnp.sum(matches * before[:, None, :], axis=2)
    offset = jnp.sum(matches * pool_offset[home_node][:, None, :], axis=2)
    target = ((arrival_rank + offset) % POOLS) * EXPERTS + expert_ids
    slot_index = arrival_rank // POOLS
    token_index = jnp.broadcast_to(jnp.arange(token_count, dtype=jnp.int32)[:, None], (token_count, TOPK))
    node_grid = jnp.broadcast_to(home_node[:, None], (token_count, TOPK))
    table = jnp.full((N_NODE, N_NODE, CAP), -1, dtype=jnp.int32)
    table = table.at[target, node_grid, slot_index].set(token_index)

    def one_node(items):
        entries, weights_gu, weights_down = items
        flat = entries.reshape(-1)
        present = flat >= 0
        rows = jnp.where(present[:, None], tokens[jnp.maximum(flat, 0)], jnp.zeros((), jnp.bfloat16))
        hidden = blocked_hidden(rows, weights_gu, width_local, FF)
        return jnp.dot(hidden, weights_down, preferred_element_type=jnp.float32).astype(jnp.bfloat16)

    outputs = lax.map(one_node, (table, gate_up, down_proj))
    pair_out = outputs[target, node_grid * CAP + slot_index]
    routed = jnp.sum(route_weight[:, :, None] * pair_out.astype(jnp.float32), axis=1)
    shared_hidden = blocked_hidden(tokens, shared_gate_up, width_local, SH)
    shared_out = jnp.dot(shared_hidden, shared_down, preferred_element_type=jnp.float32)
    return (shared_out + routed).astype(jnp.bfloat16)
```

```python
import functools
import math

import jax
import jax.numpy as jnp
from jax import lax
from jax.experimental import pallas as pl
from jax.experimental.pallas import tpu as pltpu
from jax.sharding import PartitionSpec as P

MESH = pl.DeviceIdType.MESH
MOST = 72
BLOCKS_PER_CHUNK = 2
TICKS_APART = 3
F32 = jnp.float32
BF16 = jnp.bfloat16


def dot(a, b):
    return jnp.dot(a, b, preferred_element_type=F32)


def kernel(
    cfg,
    ids_ref, wt_ref, off_ref, tok_ref, gu_hbm, dn_hbm, sgu_hbm, sdn_hbm,
    out_ref,
    gu, sgu, dn, sdn, tok2, toks, meta, codes, weights, xs, xsend, ps, pbuf, rmaj, rmin, hid, hs, obuf, rbuf, comb,
    part, prec, acc, fsend, frecv,
    part_s, part_r, loc_sem, tok_s, tok_r, meta_s, meta_r, disp_s, disp_r,
    maj_s, maj_r, min_s, min_r, gmaj_s, gmaj_r, gmin_s, gmin_r, ret_s, ret_r, sum_s, sum_r,
):
    side, nx, experts, pools, half, rows = (cfg[k] for k in ("side", "nx", "experts", "pools", "half", "rows"))
    per, apart = cfg["per"], cfg["apart"]
    tn = tok_ref.shape[0]
    width = tok_ref.shape[1]
    th = tn // 2
    chunks = side // per
    unit_cols = pbuf.shape[3]
    kept = half * side
    shift_pool, shift_side = pools.bit_length() - 1, side.bit_length() - 1

    n, l = lax.axis_index("node"), lax.axis_index("local")
    x, c = lax.div(l, 2), lax.rem(l, 2)
    z, y = lax.div(n, side), lax.rem(n, side)
    a1 = y * (1 - c) + z * c
    a2 = z * (1 - c) + y * c
    stride1 = 1 + (side - 1) * c
    stride2 = side - (side - 1) * c
    sgn = 1 - 2 * c

    def ring(i, count):
        return lax.rem(i + 2 * count, count)

    def node_at(i1, i2):
        return i1 * stride1 + i2 * stride2

    partner = (n, x * 2 + 1 - c)

    def x_peer(step):
        return (n, ring(x + step, nx) * 2 + c)

    def first_peer(step):
        return (node_at(ring(a1 + step, side), a2), l)

    def second_peer(step):
        return (node_at(a1, ring(a2 + step, side)), l)

    offsets = [0]
    for d in range(1, side // 2 + 1):
        offsets += [d, -d]
    offsets = offsets[:side]
    pending = []

    def send(src, dst, s, r, to):
        copy = pltpu.make_async_remote_copy(
            src_ref=src, dst_ref=dst, send_sem=s, recv_sem=r, device_id=to, device_id_type=MESH
        )
        copy.start()
        pending.append(copy)

    def arrived(dst, s, r):
        pltpu.make_async_remote_copy(
            src_ref=dst, dst_ref=dst, send_sem=s, recv_sem=r, device_id=partner, device_id_type=MESH
        ).wait_recv()

    barrier = pltpu.get_barrier_semaphore()
    greeted = [partner, x_peer(1), x_peer(-1)]
    greeted += [first_peer(d) for d in range(1, side)] + [second_peer(d) for d in range(1, side)]
    for to in greeted:
        pl.semaphore_signal(barrier, inc=1, device_id=to, device_id_type=MESH)

    gu_rows = pl.ds(pl.multiple_of(c * width, 16), width)
    own = [
        pltpu.make_async_copy(sgu_hbm, sgu.at[gu_rows], loc_sem.at[0]),
        pltpu.make_async_copy(gu_hbm, gu.at[gu_rows], loc_sem.at[1]),
        pltpu.make_async_copy(dn_hbm, dn.at[c], loc_sem.at[2]),
        pltpu.make_async_copy(sdn_hbm, sdn.at[c], loc_sem.at[3]),
    ]
    for copy in own:
        copy.start()

    ids, wt = ids_ref[...], wt_ref[...]
    expert = lax.broadcasted_iota(jnp.int32, (experts, tn), 0)
    named = jnp.zeros((experts, tn), F32)
    gate_weight = jnp.zeros((experts, tn), F32)
    for k in range(ids.shape[0]):
        hit = ids[k : k + 1, :] == expert
        named = named + jnp.where(hit, 1.0, 0.0)
        gate_weight = gate_weight + jnp.where(hit, wt[k : k + 1, :], 0.0)
    earlier = jnp.where(
        lax.broadcasted_iota(jnp.int32, (tn, tn), 0) < lax.broadcasted_iota(jnp.int32, (tn, tn), 1), 1.0, 0.0
    ).astype(BF16)
    rank = dot(named.astype(BF16), earlier).astype(jnp.int32)
    code = ((rank + off_ref[...]) & (pools - 1)) * 32 + (rank >> shift_pool)
    code = jnp.where(named > 0.0, code.astype(F32), -1.0)
    meta[a1] = jnp.concatenate([code, gate_weight], axis=0)
    tok2[c] = tok_ref[...]

    pl.semaphore_wait(barrier, len(greeted))

    send(tok_ref, tok2.at[c], part_s.at[0], part_r.at[0], partner)
    for d in range(1, side):
        send(meta.at[a1], meta.at[a1], meta_s.at[d - 1], meta_r.at[d - 1], first_peer(d))
    send(sgu_hbm, sgu.at[gu_rows], part_s.at[1], part_r.at[1], partner)
    send(gu_hbm, gu.at[gu_rows], part_s.at[2], part_r.at[2], partner)
    send(dn_hbm, dn.at[c], part_s.at[3], part_r.at[3], partner)
    send(sdn_hbm, sdn.at[c], part_s.at[4], part_r.at[4], partner)

    other_rows = pl.ds(pl.multiple_of((1 - c) * width, 16), width)
    arrived(tok2.at[1 - c], part_s.at[0], part_r.at[0])
    toks[a1] = jnp.concatenate([tok2[0], tok2[1]], axis=1)

    long_way, short_way = side // 2, side - 1 - side // 2

    def token_hop(h, direction, piece):
        hops = long_way if (direction > 0) == (piece == 0) else short_way
        if h > hops:
            return
        index = ring(a1 - direction * (h - 1), side)
        slot = (h - 1) * 4 + piece * 2 + (direction > 0)
        view = toks.at[index, pl.ds(piece * th, th)]
        send(view, view, tok_s.at[slot], tok_r.at[slot], first_peer(direction))

    def token_wait(h, direction, piece):
        hops = long_way if (direction > 0) == (piece == 0) else short_way
        if h > hops:
            return
        index = ring(a1 - direction * h, side)
        slot = (h - 1) * 4 + piece * 2 + (direction > 0)
        arrived(toks.at[index, pl.ds(piece * th, th)], tok_s.at[slot], tok_r.at[slot])

    ways = [(1, 0), (-1, 1), (1, 1), (-1, 0)]
    for h in range(1, long_way + 1):
        for direction, piece in ways:
            if h > 1:
                token_wait(h - 1, direction, piece)
            token_hop(h, direction, piece)

    own[0].wait()
    arrived(sgu.at[other_rows], part_s.at[1], part_r.at[1])
    mine = toks[a1, pl.ds(pl.multiple_of(c * th, 16), th), :]
    ps[...] = jnp.zeros_like(ps)

    def shared_step(q, carry):
        cols = pl.ds(pl.multiple_of(q * unit_cols, 128), unit_cols)
        ps[q, 0:th, :] = dot(mine, sgu[:, cols])
        return carry

    lax.fori_loop(0, nx, shared_step, 0)

    for d in range(1, side):
        arrived(meta.at[ring(a1 - d, side)], meta_s.at[d - 1], meta_r.at[d - 1])
    codes[...] = jnp.concatenate([meta[i, 0:experts, :] + 128.0 * i for i in range(side)], axis=1)
    weights[...] = jnp.concatenate([meta[i, experts:, :] for i in range(side)], axis=1)

    for direction, piece in ways:
        token_wait(long_way, direction, piece)

    row = lax.broadcasted_iota(jnp.int32, (rows, 1), 0)

    def matches(b):
        m = node_at(a1, ring(a2 + offsets[b], side))
        p, e = lax.div(m, experts), lax.rem(m, experts)
        want = (row & (side - 1)) * 128 + (row >> shift_side) + (p * 32 + half * c)
        want = jnp.where(row < kept, want, -5).astype(F32)
        return codes[pl.ds(e, 1), :] == want, weights[pl.ds(e, 1), :]

    flat_toks = toks[...].reshape(side * tn, 2 * width)
    for k in range(chunks):
        chosen = jnp.concatenate(
            [jnp.where(matches(k * per + i)[0], 1.0, 0.0) for i in range(per)], axis=0
        ).astype(BF16)
        picked = dot(chosen, flat_toks).astype(BF16)
        for i in range(per):
            b = k * per + i
            block = picked[i * rows : (i + 1) * rows]
            if b == 0:
                xs[0] = block
            else:
                xsend[b] = block
                send(xsend.at[b], xs.at[b], disp_s.at[b - 1], disp_r.at[b - 1], second_peer(offsets[b]))

    own[1].wait()
    arrived(gu.at[other_rows], part_s.at[2], part_r.at[2])

    hmaj, hmin = nx // 2, nx - 1 - nx // 2

    def to_x(off):
        return ring(x + sgn * off, nx)

    def start_chunk(k):
        for i in range(per):
            b = k * per + i
            if b > 0:
                arrived(xs.at[b], disp_s.at[b - 1], disp_r.at[b - 1])
        rows_in = xs[k * per : (k + 1) * per].reshape(per * rows, 2 * width)

        def step(i, carry):
            q = to_x(hmaj - i)
            cols = pl.ds(pl.multiple_of(q * unit_cols, 128), unit_cols)
            value = dot(rows_in, gu[:, cols])
            shared = ps[q, k * per * 8 : (k + 1) * per * 8, :]
            pieces = []
            for j in range(per):
                pieces += [value[j * rows : j * rows + kept], shared[j * 8 : (j + 1) * 8]]
            pbuf[k, q] = jnp.concatenate(pieces, axis=0).astype(BF16)
            return carry

        lax.fori_loop(0, nx, step, 0)
        send(pbuf.at[k, to_x(hmaj)], rmaj.at[k, 0], maj_s.at[k * hmaj], maj_r.at[k * hmaj], x_peer(sgn))
        if hmin:
            send(pbuf.at[k, to_x(-hmin)], rmin.at[k, 0], min_s.at[k * hmin], min_r.at[k * hmin], x_peer(-sgn))

    def sum_hop(k, h, hops, way, recv, s, r):
        slot = k * hops + h
        arrived(recv.at[k, h - 1], s.at[slot - 1], r.at[slot - 1])
        q = to_x(way * (hops - h))
        pbuf[k, q] = (pbuf[k, q].astype(F32) + recv[k, h - 1].astype(F32)).astype(BF16)
        send(pbuf.at[k, q], recv.at[k, h], s.at[slot], r.at[slot], x_peer(sgn * way))

    def activate(k):
        slot = k * hmaj + hmaj - 1
        arrived(rmaj.at[k, hmaj - 1], maj_s.at[slot], maj_r.at[slot])
        total = pbuf[k, x].astype(F32) + rmaj[k, hmaj - 1].astype(F32)
        if hmin:
            slot = k * hmin + hmin - 1
            arrived(rmin.at[k, hmin - 1], min_s.at[slot], min_r.at[slot])
            total = total + rmin[k, hmin - 1].astype(F32)
        wide = unit_cols // 2
        left, right = total[:, :wide], total[:, wide:]
        low = lax.broadcasted_iota(jnp.int32, left.shape, 1) < wide // 2
        gate = jnp.where(low, left, pltpu.roll(right, wide // 2, 1))
        upper = jnp.where(low, pltpu.roll(left, wide // 2, 1), right)
        hid[k, x] = (gate / (1.0 + jnp.exp(-gate)) * upper).astype(BF16)
        gather_hop(k, 1, hmaj, 1, gmaj_s, gmaj_r)
        gather_hop(k, 1, hmin, -1, gmin_s, gmin_r)

    def gather_hop(k, h, hops, way, s, r):
        if h > hops:
            return
        view = hid.at[k, to_x(-way * (h - 1))]
        slot = k * hops + h - 1
        send(view, view, s.at[slot], r.at[slot], x_peer(sgn * way))

    def gather_wait(k, h, hops, way, s, r):
        if h > hops:
            return
        slot = k * hops + h - 1
        arrived(hid.at[k, to_x(-way * h)], s.at[slot], r.at[slot])

    def finish_chunk(k):
        if k == 0:
            own[2].wait()
            arrived(dn.at[1 - c], part_s.at[3], part_r.at[3])
        hidden = jnp.concatenate([hid[k, q] for q in range(nx)], axis=1)
        both = [dot(hidden, dn[i]) for i in range(2)]
        result = jnp.concatenate(both, axis=1).astype(BF16)
        for i in range(per):
            b = k * per + i
            block = result[i * rows : (i + 1) * rows]
            if b == 0:
                rbuf[0] = block
            else:
                obuf[b] = block
                send(obuf.at[b], rbuf.at[b], ret_s.at[b - 1], ret_r.at[b - 1], second_peer(-offsets[b]))
        for i in range(per):
            b = k * per + i
            if b * 8 < th:
                top = (i + 1) * rows - 16
                hs[b * 8 : (b + 1) * 8, :] = hidden[top : top + 16].astype(F32)[8:16]

    def stage(k, s):
        if s == 0:
            start_chunk(k)
        elif s < hmaj:
            sum_hop(k, s, hmaj, 1, rmaj, maj_s, maj_r)
            if s < hmin:
                sum_hop(k, s, hmin, -1, rmin, min_s, min_r)
        elif s == hmaj:
            activate(k)
        else:
            h = s - hmaj
            gather_wait(k, h, hmaj, 1, gmaj_s, gmaj_r)
            gather_hop(k, h + 1, hmaj, 1, gmaj_s, gmaj_r)
            gather_wait(k, h, hmin, -1, gmin_s, gmin_r)
            gather_hop(k, h + 1, hmin, -1, gmin_s, gmin_r)
            if h == hmaj:
                finish_chunk(k)

    stages = 2 * hmaj + 1
    for tick in range((chunks - 1) * apart + stages):
        for k in range(chunks):
            s = tick - k * apart
            if 0 <= s < stages:
                stage(k, s)

    own[3].wait()
    arrived(sdn.at[1 - c], part_s.at[4], part_r.at[4])
    shared_hidden = hs[...].astype(BF16)
    shared_out = jnp.concatenate([dot(shared_hidden, sdn[i]) for i in range(2)], axis=1)

    for b in range(side):
        hit, weight = matches(b)
        comb[b * rows : (b + 1) * rows, :] = jnp.where(hit, weight, 0.0).astype(BF16)
    for b in range(1, side):
        arrived(rbuf.at[b], ret_s.at[b - 1], ret_r.at[b - 1])
    returned = rbuf[...].reshape(side * rows, 2 * width)
    sums = lax.dot_general(comb[...], returned, (((0,), (0,)), ((), ())), preferred_element_type=F32)
    part[...] = sums.astype(BF16).reshape(side, tn, 2 * width)
    for d in range(1, side):
        send(part.at[ring(a1 + d, side)], prec.at[d - 1], sum_s.at[d - 1], sum_r.at[d - 1], first_peer(d))
    acc[...] = part[a1].astype(F32)
    mine_rows = pl.ds(pl.multiple_of(c * th, 8), th)
    acc[mine_rows, :] = acc[mine_rows, :] + shared_out
    total = acc[...]
    for d in range(1, side):
        arrived(prec.at[d - 1], sum_s.at[d - 1], sum_r.at[d - 1])
        total = total + prec[d - 1].astype(F32)
    low, high = total[:, :width], total[:, width:]
    first = c == 0
    fsend[...] = jnp.where(first, high, low)
    send(fsend, frecv, part_s.at[5], part_r.at[5], partner)
    keep = jnp.where(first, low, high)
    arrived(frecv, part_s.at[5], part_r.at[5])
    out_ref[...] = (keep + frecv[...]).astype(BF16)
    for copy in pending:
        copy.wait_send()


def build(mesh, most):
    nodes, locals_ = mesh.shape["node"], mesh.shape["local"]
    side, nx = math.isqrt(nodes), locals_ // 2

    def shards(tokens, expert_ids, route_weight, pool_offset, gate_up, down_proj, shared_gate_up, shared_down):
        tn, width = tokens.shape
        experts = pool_offset.shape[1]
        pools = nodes // experts
        half = most // pools // 2
        rows = half * side + 8
        per = min(BLOCKS_PER_CHUNK, side)
        chunks = side // per
        two = shared_gate_up.shape[1]
        ff = two // 2
        cols = two // nx
        crows = per * rows
        hmaj, hmin = nx // 2, nx - 1 - nx // 2
        cfg = dict(
            side=side, nx=nx, experts=experts, pools=pools, half=half, rows=rows, per=per, apart=TICKS_APART
        )
        long_way = side // 2
        dma = pltpu.SemaphoreType.DMA
        scratch = [
            pltpu.VMEM((2 * width, two), BF16),
            pltpu.VMEM((2 * width, two), BF16),
            pltpu.VMEM((2, ff, width), BF16),
            pltpu.VMEM((2, ff, width), BF16),
            pltpu.VMEM((2, tn, width), BF16),
            pltpu.VMEM((side, tn, 2 * width), BF16),
            pltpu.VMEM((side, 2 * experts, tn), F32),
            pltpu.VMEM((experts, side * tn), F32),
            pltpu.VMEM((experts, side * tn), F32),
            pltpu.VMEM((side, rows, 2 * width), BF16),
            pltpu.VMEM((side, rows, 2 * width), BF16),
            pltpu.VMEM((nx, side * 8, cols), F32),
            pltpu.VMEM((chunks, nx, crows, cols), BF16),
            pltpu.VMEM((chunks, hmaj, crows, cols), BF16),
            pltpu.VMEM((chunks, max(hmin, 1), crows, cols), BF16),
            pltpu.VMEM((chunks, nx, crows, cols // 2), BF16),
            pltpu.VMEM((tn // 2, ff), F32),
            pltpu.VMEM((side, rows, 2 * width), BF16),
            pltpu.VMEM((side, rows, 2 * width), BF16),
            pltpu.VMEM((side * rows, side * tn), BF16),
            pltpu.VMEM((side, tn, 2 * width), BF16),
            pltpu.VMEM((side - 1, tn, 2 * width), BF16),
            pltpu.VMEM((tn, 2 * width), F32),
            pltpu.VMEM((tn, width), F32),
            pltpu.VMEM((tn, width), F32),
            dma((6,)), dma((6,)), dma((4,)),
            dma((4 * long_way,)), dma((4 * long_way,)),
            dma((side - 1,)), dma((side - 1,)),
            dma((side - 1,)), dma((side - 1,)),
            dma((chunks * hmaj,)), dma((chunks * hmaj,)),
            dma((chunks * max(hmin, 1),)), dma((chunks * max(hmin, 1),)),
            dma((chunks * hmaj,)), dma((chunks * hmaj,)),
            dma((chunks * max(hmin, 1),)), dma((chunks * max(hmin, 1),)),
            dma((side - 1,)), dma((side - 1,)),
            dma((side - 1,)), dma((side - 1,)),
        ]
        vmem, hbm = pl.BlockSpec(memory_space=pltpu.VMEM), pl.BlockSpec(memory_space=pl.ANY)
        return pl.pallas_call(
            functools.partial(kernel, cfg),
            out_shape=jax.ShapeDtypeStruct((tn, width), BF16),
            in_specs=[vmem] * 4 + [hbm] * 4,
            out_specs=vmem,
            scratch_shapes=scratch,
            compiler_params=pltpu.CompilerParams(
                collective_id=0, has_side_effects=True, vmem_limit_bytes=56 * 1024 * 1024
            ),
        )(
            expert_ids.T, route_weight.T, pool_offset.reshape(experts, 1), tokens,
            gate_up[0], down_proj[0], shared_gate_up, shared_down,
        )

    placed = (
        P("node", "local"),
        P("node", None),
        P("node", None),
        P("node", None),
        P("node", "local", None),
        P("node", None, "local"),
        P("local", None),
        P(None, "local"),
    )
    return jax.shard_map(
        shards, mesh=mesh, in_specs=placed, out_specs=P("node", "local"), check_vma=False
    )


def solution(mesh):
    return build(mesh, MOST)
```

```python
import functools
import math

import jax
import jax.numpy as jnp
from jax import lax
from jax.experimental import pallas as pl
from jax.experimental.pallas import tpu as pltpu
from jax.sharding import PartitionSpec as P

MESH = pl.DeviceIdType.MESH
MOST = 72
PIECES = 3
CHUNKS = {8: (1, 2, 2, 3), 4: (1, 2, 1), 2: (1, 1)}
STARTS = (0, 0, 1, 2)
DIRECT_SUM = (0, 0, 0, 0)
DIRECT_GATHER = (0, 0, 0, 0)
GROUPS = {8: (3, 1), 4: (2, 1), 2: (1, 1)}
FORWARD_LAG = 2
ADD_LAG = 3
F32 = jnp.float32
BF16 = jnp.bfloat16


def dot(a, b):
    return jnp.dot(a, b, preferred_element_type=F32)


def forward_rows(size, half):
    return -(-size * half // 16) * 16


def groups_of(side):
    groups, chunk, block = [], 0, 0
    for count in GROUPS[side]:
        size = sum(CHUNKS[side][chunk : chunk + count])
        groups.append((chunk, chunk + count - 1, block, size))
        chunk, block = chunk + count, block + size
    return groups


def dot_rows(a, b):
    return lax.dot_general(a, b, (((1,), (1,)), ((), ())), preferred_element_type=F32)


def kernel(
    cfg,
    ids_ref, wt_ref, off_ref, tok_ref, gu_hbm, dn_hbm, sgu_hbm, sdn_hbm,
    out_ref,
    gu, sgu, dn, sdn, tok2, toks, meta, gates, codes, chosen, xs, xsend, ps, pbuf, rmaj, rmin, rdir, hid, hs, obuf, rbuf,
    fwd, frow, comb, acc, fsend, frecv,
    part_s, part_r, loc_sem, tok_s, tok_r, meta_s, meta_r, disp_s, disp_r,
    maj_s, maj_r, min_s, min_r, dir_s, dir_r, gmaj_s, gmaj_r, gmin_s, gmin_r, gdir_s, gdir_r, ret_s, ret_r, fwd_s, fwd_r,
):
    side, nx, experts, pools, half, rows = (cfg[k] for k in ("side", "nx", "experts", "pools", "half", "rows"))
    sizes = CHUNKS[side]
    chunks = len(sizes)
    first_block = [sum(sizes[:k]) for k in range(chunks)]
    groups = groups_of(side)
    lengths = [forward_rows(group[3], half) for group in groups]
    first_row = [sum(lengths[:g]) for g in range(len(groups))]
    tn = tok_ref.shape[0]
    width = tok_ref.shape[1]
    th = tn // 2
    unit_cols = pbuf.shape[2]
    kept = half * side
    shift_pool, shift_side = pools.bit_length() - 1, side.bit_length() - 1

    n, l = lax.axis_index("node"), lax.axis_index("local")
    x, c = lax.div(l, 2), lax.rem(l, 2)
    z, y = lax.div(n, side), lax.rem(n, side)
    a1 = y * (1 - c) + z * c
    a2 = z * (1 - c) + y * c
    stride1 = 1 + (side - 1) * c
    stride2 = side - (side - 1) * c
    sgn = 1 - 2 * c

    def ring(i, count):
        return lax.rem(i + 2 * count, count)

    def node_at(i1, i2):
        return i1 * stride1 + i2 * stride2

    partner = (n, x * 2 + 1 - c)

    def x_peer(step):
        return (n, ring(x + step, nx) * 2 + c)

    def first_peer(step):
        return (node_at(ring(a1 + step, side), a2), l)

    def second_peer(step):
        return (node_at(a1, ring(a2 + step, side)), l)

    offsets = [0]
    for d in range(1, side // 2 + 1):
        offsets += [d, -d]
    offsets = offsets[:side]
    pending = []

    def send(src, dst, s, r, to):
        copy = pltpu.make_async_remote_copy(
            src_ref=src, dst_ref=dst, send_sem=s, recv_sem=r, device_id=to, device_id_type=MESH
        )
        copy.start()
        pending.append(copy)

    def arrived(dst, s, r):
        pltpu.make_async_remote_copy(
            src_ref=dst, dst_ref=dst, send_sem=s, recv_sem=r, device_id=partner, device_id_type=MESH
        ).wait_recv()

    barrier = pltpu.get_barrier_semaphore()
    greeted = [partner] + [x_peer(d) for d in range(1, nx)]
    greeted += [first_peer(d) for d in range(1, side)] + [second_peer(d) for d in range(1, side)]
    for to in greeted:
        pl.semaphore_signal(barrier, inc=1, device_id=to, device_id_type=MESH)

    gu_rows = pl.ds(pl.multiple_of(c * width, 16), width)
    own = [
        pltpu.make_async_copy(sgu_hbm, sgu.at[gu_rows], loc_sem.at[0]),
        pltpu.make_async_copy(gu_hbm, gu.at[gu_rows], loc_sem.at[1]),
        pltpu.make_async_copy(dn_hbm, dn.at[gu_rows], loc_sem.at[2]),
        pltpu.make_async_copy(sdn_hbm, sdn.at[gu_rows], loc_sem.at[3]),
    ]
    for copy in own:
        copy.start()

    ids, wt = ids_ref[...], wt_ref[...]
    expert = lax.broadcasted_iota(jnp.int32, (experts, tn), 0)
    named = jnp.zeros((experts, tn), F32)
    gate_weight = jnp.zeros((experts, tn), F32)
    for k in range(ids.shape[0]):
        hit = ids[k : k + 1, :] == expert
        named = named + jnp.where(hit, 1.0, 0.0)
        gate_weight = gate_weight + jnp.where(hit, wt[k : k + 1, :], 0.0)
    earlier = jnp.where(
        lax.broadcasted_iota(jnp.int32, (tn, tn), 0) < lax.broadcasted_iota(jnp.int32, (tn, tn), 1), 1.0, 0.0
    ).astype(BF16)
    rank = dot(named.astype(BF16), earlier).astype(jnp.int32)
    diagonal = lax.broadcasted_iota(jnp.int32, (experts, experts), 0) == lax.broadcasted_iota(
        jnp.int32, (experts, experts), 1
    )
    offset = jnp.sum(jnp.where(diagonal, off_ref[...], 0), axis=1, keepdims=True)
    code = ((rank + offset) & (pools - 1)) * 32 + (rank >> shift_pool)
    code = jnp.where(named > 0.0, code.astype(F32), -1.0)
    meta[a1] = code
    gates[...] = gate_weight
    tok2[c] = tok_ref[...]

    pl.semaphore_wait(barrier, len(greeted))

    send(tok_ref, tok2.at[c], part_s.at[0], part_r.at[0], partner)

    other_rows = pl.ds(pl.multiple_of((1 - c) * width, 16), width)
    arrived(tok2.at[1 - c], part_s.at[0], part_r.at[0])
    toks[a1] = jnp.concatenate([tok2[0], tok2[1]], axis=1)

    long_way, short_way = side // 2, side - 1 - side // 2

    cut = tn // PIECES

    def token_hop(h, direction, piece):
        hops = long_way if (direction > 0) == (piece % 2 == 0) else short_way
        if h > hops:
            return
        index = ring(a1 - direction * (h - 1), side)
        slot = ((h - 1) * PIECES + piece) * 2 + (direction > 0)
        view = toks.at[index, pl.ds(piece * cut, cut)]
        send(view, view, tok_s.at[slot], tok_r.at[slot], first_peer(direction))

    def token_wait(h, direction, piece):
        hops = long_way if (direction > 0) == (piece % 2 == 0) else short_way
        if h > hops:
            return
        index = ring(a1 - direction * h, side)
        slot = ((h - 1) * PIECES + piece) * 2 + (direction > 0)
        arrived(toks.at[index, pl.ds(piece * cut, cut)], tok_s.at[slot], tok_r.at[slot])

    ways = [(way, piece) for piece in range(PIECES) for way in (1, -1)]
    for h in range(1, long_way + 1):
        for direction, piece in ways:
            if h > 1:
                token_wait(h - 1, direction, piece)
            token_hop(h, direction, piece)
        if h == 1:
            for d in range(1, side):
                send(meta.at[a1], meta.at[a1], meta_s.at[d - 1], meta_r.at[d - 1], first_peer(d))
        if h == max(1, long_way - 2):
            send(gu_hbm, gu.at[gu_rows], part_s.at[2], part_r.at[2], partner)

    for d in range(1, side):
        arrived(meta.at[ring(a1 - d, side)], meta_s.at[d - 1], meta_r.at[d - 1])
    codes[...] = jnp.concatenate([meta[i] + 128.0 * i for i in range(side)], axis=1)
    row = lax.broadcasted_iota(jnp.int32, (rows, 1), 0)
    for b in range(side):
        m = node_at(a1, ring(a2 + offsets[b], side))
        p, e = lax.div(m, experts), lax.rem(m, experts)
        want = (row & (side - 1)) * 128 + (row >> shift_side) + (p * 32 + half * c)
        want = jnp.where(row < kept, want, -5).astype(F32)
        chosen[b * rows : (b + 1) * rows, :] = jnp.where(codes[pl.ds(e, 1), :] == want, 1.0, 0.0).astype(BF16)

    for direction, piece in ways:
        token_wait(long_way, direction, piece)

    def rows_of(k):
        return slice(first_block[k] * rows, (first_block[k] + sizes[k]) * rows)

    def span(k):
        return pl.ds(first_block[k] * rows, sizes[k] * rows)

    def one(b):
        return pl.ds(b * rows, rows)

    near = min(3, side)
    for low, high in ((1, near), (near, side), (0, 1)):
        if low == high:
            continue
        picked = dot(chosen[low * rows : high * rows, :], toks[...].reshape(side * tn, 2 * width)).astype(BF16)
        for b in range(low, high):
            block = picked[(b - low) * rows : (b - low + 1) * rows]
            if b == 0:
                xs[0:rows, :] = block
            else:
                xsend[b * rows : (b + 1) * rows, :] = block
                send(xsend.at[one(b)], xs.at[one(b)], disp_s.at[b - 1], disp_r.at[b - 1], second_peer(offsets[b]))

    def shared_start():
        own[0].wait()
        arrived(sgu.at[other_rows], part_s.at[1], part_r.at[1])
        mine = toks[a1, pl.ds(pl.multiple_of(c * th, 16), th), :]

        def shared_step(q, carry):
            cols = pl.ds(pl.multiple_of(q * unit_cols, 128), unit_cols)
            ps[q] = dot(mine, sgu[:, cols])
            return carry

        lax.fori_loop(0, nx, shared_step, 0)

    own[1].wait()
    arrived(gu.at[other_rows], part_s.at[2], part_r.at[2])
    send(sgu_hbm, sgu.at[gu_rows], part_s.at[1], part_r.at[1], partner)

    hmaj, hmin = nx // 2, nx - 1 - nx // 2
    first_shared = side - th // 8
    first_shared_chunk = [k for k in range(chunks) if first_block[k] + sizes[k] > first_shared][0]

    def to_x(off):
        return ring(x + sgn * off, nx)

    def start_chunk(k):
        for i in range(sizes[k]):
            b = first_block[k] + i
            if b > 0:
                arrived(xs.at[one(b)], disp_s.at[b - 1], disp_r.at[b - 1])
        if k == first_shared_chunk:
            shared_start()
        rows_in = xs[rows_of(k), :]

        def step(i, carry):
            q = to_x(hmaj - i)
            cols = pl.ds(pl.multiple_of(q * unit_cols, 128), unit_cols)
            value = dot(rows_in, gu[:, cols])
            pieces = []
            for j in range(sizes[k]):
                number = first_block[k] + j - first_shared
                shared = value[j * rows + kept : (j + 1) * rows]
                if number >= 0:
                    shared = ps[q, number * 8 : (number + 1) * 8, :]
                pieces += [value[j * rows : j * rows + kept], shared]
            pbuf[q, rows_of(k), :] = jnp.concatenate(pieces, axis=0).astype(BF16)
            return carry

        lax.fori_loop(0, nx, step, 0)
        if k == 0:
            send(dn_hbm, dn.at[gu_rows], part_s.at[3], part_r.at[3], partner)
            send(sdn_hbm, sdn.at[gu_rows], part_s.at[4], part_r.at[4], partner)
        if DIRECT_SUM[k]:
            for d in range(1, nx):
                slot = k * (nx - 1) + d - 1
                send(pbuf.at[ring(x + d, nx), span(k)], rdir.at[d - 1, span(k)], dir_s.at[slot], dir_r.at[slot], x_peer(d))
        else:
            sum_send(k, 0, hmaj, 1, rmaj, maj_s, maj_r)
            sum_send(k, 0, hmin, -1, rmin, min_s, min_r)

    def sum_send(k, h, hops, way, recv, s, r):
        if h < hops:
            slot = k * hops + h
            view = pbuf.at[to_x(way * (hops - h)), span(k)]
            send(view, recv.at[h, span(k)], s.at[slot], r.at[slot], x_peer(sgn * way))

    def sum_hop(k, h, hops, way, recv, s, r):
        if h < hops:
            slot = k * hops + h
            arrived(recv.at[h - 1, span(k)], s.at[slot - 1], r.at[slot - 1])
            q = to_x(way * (hops - h))
            value = pbuf[q, rows_of(k), :].astype(F32) + recv[h - 1, rows_of(k), :].astype(F32)
            pbuf[q, rows_of(k), :] = value.astype(BF16)
            sum_send(k, h, hops, way, recv, s, r)

    def sum_hops(k, h):
        sum_hop(k, h, hmaj, 1, rmaj, maj_s, maj_r)
        sum_hop(k, h, hmin, -1, rmin, min_s, min_r)

    def activate(k):
        total = pbuf[x, rows_of(k), :].astype(F32)
        if DIRECT_SUM[k]:
            for d in range(1, nx):
                slot = k * (nx - 1) + d - 1
                arrived(rdir.at[d - 1, span(k)], dir_s.at[slot], dir_r.at[slot])
                total = total + rdir[d - 1, rows_of(k), :].astype(F32)
        else:
            for hops, recv, s, r in ((hmaj, rmaj, maj_s, maj_r), (hmin, rmin, min_s, min_r)):
                if hops:
                    slot = k * hops + hops - 1
                    arrived(recv.at[hops - 1, span(k)], s.at[slot], r.at[slot])
                    total = total + recv[hops - 1, rows_of(k), :].astype(F32)
        wide = unit_cols // 2
        left, right = total[:, :wide], total[:, wide:]
        low = lax.broadcasted_iota(jnp.int32, left.shape, 1) < wide // 2
        gate = jnp.where(low, left, pltpu.roll(right, wide // 2, 1))
        upper = jnp.where(low, pltpu.roll(left, wide // 2, 1), right)
        hid[x, rows_of(k), :] = (gate / (1.0 + jnp.exp(-gate)) * upper).astype(BF16)
        if DIRECT_GATHER[k]:
            view = hid.at[x, span(k)]
            for d in range(1, nx):
                slot = k * (nx - 1) + d - 1
                send(view, view, gdir_s.at[slot], gdir_r.at[slot], x_peer(d))
        else:
            gather_hop(k, 1, hmaj, 1, gmaj_s, gmaj_r)
            gather_hop(k, 1, hmin, -1, gmin_s, gmin_r)

    def gather_hop(k, h, hops, way, s, r):
        if h <= hops:
            view = hid.at[to_x(-way * (h - 1)), span(k)]
            slot = k * hops + h - 1
            send(view, view, s.at[slot], r.at[slot], x_peer(sgn * way))

    def gather_wait(k, h, hops, way, s, r):
        if h <= hops:
            slot = k * hops + h - 1
            arrived(hid.at[to_x(-way * h), span(k)], s.at[slot], r.at[slot])

    def gather_hops(k, h):
        gather_wait(k, h, hmaj, 1, gmaj_s, gmaj_r)
        gather_hop(k, h + 1, hmaj, 1, gmaj_s, gmaj_r)
        gather_wait(k, h, hmin, -1, gmin_s, gmin_r)
        gather_hop(k, h + 1, hmin, -1, gmin_s, gmin_r)

    def finish_chunk(k):
        if DIRECT_GATHER[k]:
            for d in range(1, nx):
                slot = k * (nx - 1) + d - 1
                arrived(hid.at[ring(x - d, nx), span(k)], gdir_s.at[slot], gdir_r.at[slot])
        else:
            gather_hops(k, hmaj)
        if k == 0:
            own[2].wait()
            arrived(dn.at[other_rows], part_s.at[3], part_r.at[3])
        hidden = jnp.concatenate([hid[q, rows_of(k), :] for q in range(nx)], axis=1)
        result = dot_rows(hidden, dn[...]).astype(BF16)
        for i in range(sizes[k]):
            b = first_block[k] + i
            block = result[i * rows : (i + 1) * rows]
            if b == 0:
                rbuf[0:rows, :] = block
            else:
                obuf[b * rows : (b + 1) * rows, :] = block
                send(obuf.at[one(b)], rbuf.at[one(b)], ret_s.at[b - 1], ret_r.at[b - 1], second_peer(-offsets[b]))
        for i in range(sizes[k]):
            number = first_block[k] + i - first_shared
            if number >= 0:
                top = (i + 1) * rows - 16
                hs[number * 8 : (number + 1) * 8, :] = hidden[top : top + 16].astype(F32)[8:16]

    def place(g, index):
        node_index, which = jnp.zeros_like(index), jnp.zeros_like(index)
        for i in range(1, side):
            node_index = node_index + jnp.where(index >= i * lengths[g], 1, 0)
        number = index - node_index * lengths[g]
        for i in range(1, groups[g][3]):
            which = which + jnp.where(number >= i * half, 1, 0)
        return node_index, number < groups[g][3] * half, which, number - which * half

    def forward_span(g):
        return pl.ds(first_row[g], lengths[g])

    def forward_group(g):
        _, _, block, size = groups[g]
        for b in range(block, block + size):
            if b > 0:
                arrived(rbuf.at[one(b)], ret_s.at[b - 1], ret_r.at[b - 1])
        length = lengths[g]
        shape = (side * length, size * rows)
        node_index, used, which, slot = place(g, lax.broadcasted_iota(jnp.int32, (shape[0], 1), 0))
        source = jnp.where(used, which * rows + slot * side + node_index, -1)
        moved = jnp.where(lax.broadcasted_iota(jnp.int32, shape, 1) == source, 1.0, 0.0).astype(BF16)
        result = dot(moved, rbuf[block * rows : (block + size) * rows, :]).astype(BF16)
        for i in range(side):
            fwd[i, first_row[g] : first_row[g] + length, :] = result[i * length : (i + 1) * length]
        for d in range(1, side):
            slot = g * (side - 1) + d - 1
            send(
                fwd.at[ring(a1 + d, side), forward_span(g)], frow.at[a1, forward_span(g)],
                fwd_s.at[slot], fwd_r.at[slot], first_peer(d),
            )
        frow[a1, first_row[g] : first_row[g] + length, :] = fwd[a1, first_row[g] : first_row[g] + length, :]

    def weigh_group(g):
        _, _, block, size = groups[g]
        length = lengths[g]
        node_index, used, which, slot = place(g, lax.broadcasted_iota(jnp.int32, (1, side * length), 1))
        shift = jnp.zeros_like(which)
        for i in range(size):
            shift = jnp.where(which == i, offsets[block + i], shift)
        second = (a2 + shift + side) & (side - 1)
        m = node_index * stride1 + second * stride2
        want = (m >> (experts.bit_length() - 1)) * 32 + slot + half * c
        want = jnp.where(used, want, -5).astype(F32)
        chosen_expert = lax.broadcasted_iota(jnp.int32, (experts, side * length), 0) == (m & (experts - 1))
        chosen_expert = jnp.where(chosen_expert, 1.0, 0.0).astype(BF16)
        ends = (((0,), (0,)), ((), ()))
        found = lax.dot_general(meta[a1].astype(BF16), chosen_expert, ends, preferred_element_type=F32)
        weight = lax.dot_general(gates[...].astype(BF16), chosen_expert, ends, preferred_element_type=F32)
        comb[:, first_row[g] * side : (first_row[g] + length) * side] = jnp.where(found == want, weight, 0.0).astype(BF16)

    def add_group(g):
        length = lengths[g]
        for d in range(1, side):
            slot = g * (side - 1) + d - 1
            arrived(frow.at[ring(a1 - d, side), forward_span(g)], fwd_s.at[slot], fwd_r.at[slot])
        landed = frow[:, first_row[g] : first_row[g] + length, :].reshape(side * length, 2 * width)
        acc[...] += dot(comb[:, first_row[g] * side : (first_row[g] + length) * side], landed)

    def shared_finish():
        own[3].wait()
        arrived(sdn.at[other_rows], part_s.at[4], part_r.at[4])
        mine_rows = pl.ds(pl.multiple_of(c * th, 8), th)
        acc[mine_rows, :] += dot_rows(hs[...].astype(BF16), sdn[...])

    schedule = []
    for k in range(chunks):
        steps = [start_chunk]
        if not DIRECT_SUM[k]:
            steps += [functools.partial(lambda h, k: sum_hops(k, h), h) for h in range(1, hmaj)]
        steps += [activate]
        if not DIRECT_GATHER[k]:
            steps += [functools.partial(lambda h, k: gather_hops(k, h), h) for h in range(1, hmaj)]
        steps += [finish_chunk]
        for i, f in enumerate(steps):
            schedule.append((STARTS[k] + i, k, f))
        finish = STARTS[k] + len(steps) - 1
        for g, group in enumerate(groups):
            if group[1] == k:
                schedule.append((STARTS[0] + 2 + g, chunks, functools.partial(lambda g, _: weigh_group(g), g)))
                schedule.append((finish + FORWARD_LAG, k, functools.partial(lambda g, _: forward_group(g), g)))
                schedule.append((finish + ADD_LAG, k, functools.partial(lambda g, _: add_group(g), g)))
    schedule.sort(key=lambda item: item[:2])
    acc[...] = jnp.zeros_like(acc)
    for _, k, f in schedule:
        f(k)
        if f is finish_chunk and k == chunks - 1:
            shared_finish()
    total = acc[...]
    low, high = total[:, :width], total[:, width:]
    first = c == 0
    fsend[...] = jnp.where(first, high, low)
    send(fsend, frecv, part_s.at[5], part_r.at[5], partner)
    keep = jnp.where(first, low, high)
    arrived(frecv, part_s.at[5], part_r.at[5])
    out_ref[...] = (keep + frecv[...]).astype(BF16)
    for copy in pending:
        copy.wait_send()


def build(mesh, most):
    nodes, locals_ = mesh.shape["node"], mesh.shape["local"]
    side, nx = math.isqrt(nodes), locals_ // 2

    def shards(tokens, expert_ids, route_weight, pool_offset, gate_up, down_proj, shared_gate_up, shared_down):
        tn, width = tokens.shape
        experts = pool_offset.shape[1]
        pools = nodes // experts
        half = most // pools // 2
        rows = half * side + 8
        sizes = CHUNKS[side]
        chunks = len(sizes)
        forwarded = sum(forward_rows(group[3], half) for group in groups_of(side))
        parcels = len(GROUPS[side]) * (side - 1)
        two = shared_gate_up.shape[1]
        ff = two // 2
        cols = two // nx
        every = side * rows
        hmaj, hmin = nx // 2, max(nx - 1 - nx // 2, 1)
        cfg = dict(side=side, nx=nx, experts=experts, pools=pools, half=half, rows=rows)
        long_way = side // 2
        dma = pltpu.SemaphoreType.DMA
        scratch = [
            pltpu.VMEM((2 * width, two), BF16),
            pltpu.VMEM((2 * width, two), BF16),
            pltpu.VMEM((2 * width, ff), BF16),
            pltpu.VMEM((2 * width, ff), BF16),
            pltpu.VMEM((2, tn, width), BF16),
            pltpu.VMEM((side, tn, 2 * width), BF16),
            pltpu.VMEM((side, experts, tn), F32),
            pltpu.VMEM((experts, tn), F32),
            pltpu.VMEM((experts, side * tn), F32),
            pltpu.VMEM((every, side * tn), BF16),
            pltpu.VMEM((every, 2 * width), BF16),
            pltpu.VMEM((every, 2 * width), BF16),
            pltpu.VMEM((nx, tn // 2, cols), F32),
            pltpu.VMEM((nx, every, cols), BF16),
            pltpu.VMEM((hmaj, every, cols), BF16),
            pltpu.VMEM((hmin, every, cols), BF16),
            pltpu.VMEM((nx - 1, every, cols), BF16),
            pltpu.VMEM((nx, every, cols // 2), BF16),
            pltpu.VMEM((tn // 2, ff), F32),
            pltpu.VMEM((every, 2 * width), BF16),
            pltpu.VMEM((every, 2 * width), BF16),
            pltpu.VMEM((side, forwarded, 2 * width), BF16),
            pltpu.VMEM((side, forwarded, 2 * width), BF16),
            pltpu.VMEM((tn, side * forwarded), BF16),
            pltpu.VMEM((tn, 2 * width), F32),
            pltpu.VMEM((tn, width), F32),
            pltpu.VMEM((tn, width), F32),
            dma((6,)), dma((6,)), dma((4,)),
            dma((2 * PIECES * long_way,)), dma((2 * PIECES * long_way,)),
            dma((side - 1,)), dma((side - 1,)),
            dma((side - 1,)), dma((side - 1,)),
            dma((chunks * hmaj,)), dma((chunks * hmaj,)),
            dma((chunks * hmin,)), dma((chunks * hmin,)),
            dma((chunks * (nx - 1),)), dma((chunks * (nx - 1),)),
            dma((chunks * hmaj,)), dma((chunks * hmaj,)),
            dma((chunks * hmin,)), dma((chunks * hmin,)),
            dma((chunks * (nx - 1),)), dma((chunks * (nx - 1),)),
            dma((side - 1,)), dma((side - 1,)),
            dma((parcels,)), dma((parcels,)),
        ]
        vmem, hbm = pl.BlockSpec(memory_space=pltpu.VMEM), pl.BlockSpec(memory_space=pl.ANY)
        return pl.pallas_call(
            functools.partial(kernel, cfg),
            out_shape=jax.ShapeDtypeStruct((tn, width), BF16),
            in_specs=[vmem] * 4 + [hbm] * 4,
            out_specs=vmem,
            scratch_shapes=scratch,
            compiler_params=pltpu.CompilerParams(
                collective_id=0, has_side_effects=True, vmem_limit_bytes=56 * 1024 * 1024
            ),
        )(
            expert_ids.T, route_weight.T, pool_offset, tokens,
            gate_up[0], down_proj[0].T, shared_gate_up, shared_down.T,
        )

    placed = (
        P("node", "local"),
        P("node", None),
        P("node", None),
        P("node", None),
        P("node", "local", None),
        P("node", None, "local"),
        P("local", None),
        P(None, "local"),
    )
    return jax.shard_map(
        shards, mesh=mesh, in_specs=placed, out_specs=P("node", "local"), check_vma=False
    )


def solution(mesh):
    return build(mesh, MOST)
```

```python
import functools
import math

import jax
import jax.numpy as jnp
from jax import lax
from jax.experimental import pallas as pl
from jax.experimental.pallas import tpu as pltpu
from jax.sharding import PartitionSpec as P

MESH = pl.DeviceIdType.MESH
MOST = 72
OFFSETS = {8: (0, 1, -1, 3, -3, 4, 2, -2), 4: (0, 1, -1, 2), 2: (0, 1)}
PIECES = 3
CHUNKS = {8: (1, 2, 3, 2), 4: (1, 2, 1), 2: (1, 1)}
STARTS = (0, 0, 1, 1)
DIRECT_SUM = (0, 0, 0, 0)
DIRECT_GATHER = (0, 0, 0, 0)
GROUPS = {8: (3, 1), 4: (2, 1), 2: (1, 1)}
FORWARD_LAG = 2
ADD_LAG = 3
F32 = jnp.float32
BF16 = jnp.bfloat16


def dot(a, b):
    return jnp.dot(a, b, preferred_element_type=F32)


def forward_rows(size, half):
    return -(-size * half // 16) * 16


def groups_of(side):
    groups, chunk, block = [], 0, 0
    for count in GROUPS[side]:
        size = sum(CHUNKS[side][chunk : chunk + count])
        groups.append((chunk, chunk + count - 1, block, size))
        chunk, block = chunk + count, block + size
    return groups


def dot_rows(a, b):
    return lax.dot_general(a, b, (((1,), (1,)), ((), ())), preferred_element_type=F32)


def kernel(
    cfg,
    ids_ref, wt_ref, off_ref, tok_ref, gu_hbm, dn_hbm, sgu_hbm, sdn_hbm,
    out_ref,
    gu, sgu, dn, sdn, tok2, toks, meta, gates, codes, chosen, xs, xsend, ps, pbuf, rmaj, rmin, rdir, hid, hs, obuf, rbuf,
    fwd, frow, comb, acc, fsend, frecv,
    part_s, part_r, loc_sem, tok_s, tok_r, meta_s, meta_r, disp_s, disp_r,
    maj_s, maj_r, min_s, min_r, dir_s, dir_r, gmaj_s, gmaj_r, gmin_s, gmin_r, gdir_s, gdir_r, ret_s, ret_r, fwd_s, fwd_r,
):
    side, nx, experts, pools, half, rows = (cfg[k] for k in ("side", "nx", "experts", "pools", "half", "rows"))
    sizes = CHUNKS[side]
    chunks = len(sizes)
    first_block = [sum(sizes[:k]) for k in range(chunks)]
    groups = groups_of(side)
    lengths = [forward_rows(group[3], half) for group in groups]
    first_row = [sum(lengths[:g]) for g in range(len(groups))]
    tn = tok_ref.shape[0]
    width = tok_ref.shape[1]
    th = tn // 2
    unit_cols = pbuf.shape[2]
    kept = half * side
    shift_pool, shift_side = pools.bit_length() - 1, side.bit_length() - 1

    n, l = lax.axis_index("node"), lax.axis_index("local")
    x, c = lax.div(l, 2), lax.rem(l, 2)
    z, y = lax.div(n, side), lax.rem(n, side)
    a1 = y * (1 - c) + z * c
    a2 = z * (1 - c) + y * c
    stride1 = 1 + (side - 1) * c
    stride2 = side - (side - 1) * c
    sgn = 1 - 2 * c

    def ring(i, count):
        return lax.rem(i + 2 * count, count)

    def node_at(i1, i2):
        return i1 * stride1 + i2 * stride2

    partner = (n, x * 2 + 1 - c)

    def x_peer(step):
        return (n, ring(x + step, nx) * 2 + c)

    def first_peer(step):
        return (node_at(ring(a1 + step, side), a2), l)

    def second_peer(step):
        return (node_at(a1, ring(a2 + step, side)), l)

    offsets = OFFSETS[side]
    pending = []

    def send(src, dst, s, r, to):
        copy = pltpu.make_async_remote_copy(
            src_ref=src, dst_ref=dst, send_sem=s, recv_sem=r, device_id=to, device_id_type=MESH
        )
        copy.start()
        pending.append(copy)

    def arrived(dst, s, r):
        pltpu.make_async_remote_copy(
            src_ref=dst, dst_ref=dst, send_sem=s, recv_sem=r, device_id=partner, device_id_type=MESH
        ).wait_recv()

    barrier = pltpu.get_barrier_semaphore()
    greeted = [partner] + [x_peer(d) for d in range(1, nx)]
    greeted += [first_peer(d) for d in range(1, side)] + [second_peer(d) for d in range(1, side)]
    for to in greeted:
        pl.semaphore_signal(barrier, inc=1, device_id=to, device_id_type=MESH)

    gu_rows = pl.ds(pl.multiple_of(c * width, 16), width)
    own = [
        pltpu.make_async_copy(sgu_hbm, sgu.at[gu_rows], loc_sem.at[0]),
        pltpu.make_async_copy(gu_hbm, gu.at[gu_rows], loc_sem.at[1]),
        pltpu.make_async_copy(dn_hbm, dn.at[gu_rows], loc_sem.at[2]),
        pltpu.make_async_copy(sdn_hbm, sdn.at[gu_rows], loc_sem.at[3]),
    ]
    for copy in own:
        copy.start()

    ids, wt = ids_ref[...], wt_ref[...]
    expert = lax.broadcasted_iota(jnp.int32, (experts, tn), 0)
    named = jnp.zeros((experts, tn), F32)
    gate_weight = jnp.zeros((experts, tn), F32)
    for k in range(ids.shape[0]):
        hit = ids[k : k + 1, :] == expert
        named = named + jnp.where(hit, 1.0, 0.0)
        gate_weight = gate_weight + jnp.where(hit, wt[k : k + 1, :], 0.0)
    earlier = jnp.where(
        lax.broadcasted_iota(jnp.int32, (tn, tn), 0) < lax.broadcasted_iota(jnp.int32, (tn, tn), 1), 1.0, 0.0
    ).astype(BF16)
    rank = dot(named.astype(BF16), earlier).astype(jnp.int32)
    diagonal = lax.broadcasted_iota(jnp.int32, (experts, experts), 0) == lax.broadcasted_iota(
        jnp.int32, (experts, experts), 1
    )
    offset = jnp.sum(jnp.where(diagonal, off_ref[...], 0), axis=1, keepdims=True)
    code = ((rank + offset) & (pools - 1)) * 32 + (rank >> shift_pool)
    code = jnp.where(named > 0.0, code.astype(F32), -1.0)
    meta[a1] = code
    gates[...] = gate_weight
    tok2[c] = tok_ref[...]

    pl.semaphore_wait(barrier, len(greeted))

    send(tok_ref, tok2.at[c], part_s.at[0], part_r.at[0], partner)

    other_rows = pl.ds(pl.multiple_of((1 - c) * width, 16), width)
    arrived(tok2.at[1 - c], part_s.at[0], part_r.at[0])
    toks[a1] = jnp.concatenate([tok2[0], tok2[1]], axis=1)

    long_way, short_way = side // 2, side - 1 - side // 2

    cut = tn // PIECES

    def token_hop(h, direction, piece):
        hops = long_way if (direction > 0) == (piece % 2 == 0) else short_way
        if h > hops:
            return
        index = ring(a1 - direction * (h - 1), side)
        slot = ((h - 1) * PIECES + piece) * 2 + (direction > 0)
        view = toks.at[index, pl.ds(piece * cut, cut)]
        send(view, view, tok_s.at[slot], tok_r.at[slot], first_peer(direction))

    def token_wait(h, direction, piece):
        hops = long_way if (direction > 0) == (piece % 2 == 0) else short_way
        if h > hops:
            return
        index = ring(a1 - direction * h, side)
        slot = ((h - 1) * PIECES + piece) * 2 + (direction > 0)
        arrived(toks.at[index, pl.ds(piece * cut, cut)], tok_s.at[slot], tok_r.at[slot])

    ways = [(way, piece) for piece in range(PIECES) for way in (1, -1)]
    for h in range(1, long_way + 1):
        for direction, piece in ways:
            if h > 1:
                token_wait(h - 1, direction, piece)
            token_hop(h, direction, piece)
        if h == 1:
            for d in range(1, side):
                send(meta.at[a1], meta.at[a1], meta_s.at[d - 1], meta_r.at[d - 1], first_peer(d))
        if h == max(1, long_way - 2):
            send(gu_hbm, gu.at[gu_rows], part_s.at[2], part_r.at[2], partner)

    for d in range(1, side):
        arrived(meta.at[ring(a1 - d, side)], meta_s.at[d - 1], meta_r.at[d - 1])
    codes[...] = jnp.concatenate([meta[i] + 128.0 * i for i in range(side)], axis=1)
    row = lax.broadcasted_iota(jnp.int32, (rows, 1), 0)
    for b in range(side):
        m = node_at(a1, ring(a2 + offsets[b], side))
        p, e = lax.div(m, experts), lax.rem(m, experts)
        want = (row & (side - 1)) * 128 + (row >> shift_side) + (p * 32 + half * c)
        want = jnp.where(row < kept, want, -5).astype(F32)
        chosen[b * rows : (b + 1) * rows, :] = jnp.where(codes[pl.ds(e, 1), :] == want, 1.0, 0.0).astype(BF16)

    for direction, piece in ways:
        token_wait(long_way, direction, piece)

    def rows_of(k):
        return slice(first_block[k] * rows, (first_block[k] + sizes[k]) * rows)

    def span(k):
        return pl.ds(first_block[k] * rows, sizes[k] * rows)

    def one(b):
        return pl.ds(b * rows, rows)

    near = min(3, side)
    for low, high in ((1, near), (near, side), (0, 1)):
        if low == high:
            continue
        picked = dot(chosen[low * rows : high * rows, :], toks[...].reshape(side * tn, 2 * width)).astype(BF16)
        for b in range(low, high):
            block = picked[(b - low) * rows : (b - low + 1) * rows]
            if b == 0:
                xs[0:rows, :] = block
            else:
                xsend[b * rows : (b + 1) * rows, :] = block
                send(xsend.at[one(b)], xs.at[one(b)], disp_s.at[b - 1], disp_r.at[b - 1], second_peer(offsets[b]))

    def shared_start():
        own[0].wait()
        arrived(sgu.at[other_rows], part_s.at[1], part_r.at[1])
        mine = toks[a1, pl.ds(pl.multiple_of(c * th, 16), th), :]

        def shared_step(q, carry):
            cols = pl.ds(pl.multiple_of(q * unit_cols, 128), unit_cols)
            ps[q] = dot(mine, sgu[:, cols])
            return carry

        lax.fori_loop(0, nx, shared_step, 0)

    own[1].wait()
    arrived(gu.at[other_rows], part_s.at[2], part_r.at[2])
    send(sgu_hbm, sgu.at[gu_rows], part_s.at[1], part_r.at[1], partner)

    hmaj, hmin = nx // 2, nx - 1 - nx // 2
    first_shared = side - th // 8
    first_shared_chunk = [k for k in range(chunks) if first_block[k] + sizes[k] > first_shared][0]

    def to_x(off):
        return ring(x + sgn * off, nx)

    def start_chunk(k):
        for i in range(sizes[k]):
            b = first_block[k] + i
            if b > 0:
                arrived(xs.at[one(b)], disp_s.at[b - 1], disp_r.at[b - 1])
        if k == first_shared_chunk:
            shared_start()
        rows_in = xs[rows_of(k), :]

        def step(i, carry):
            q = to_x(hmaj - i)
            cols = pl.ds(pl.multiple_of(q * unit_cols, 128), unit_cols)
            value = dot(rows_in, gu[:, cols])
            pieces = []
            for j in range(sizes[k]):
                number = first_block[k] + j - first_shared
                shared = value[j * rows + kept : (j + 1) * rows]
                if number >= 0:
                    shared = ps[q, number * 8 : (number + 1) * 8, :]
                pieces += [value[j * rows : j * rows + kept], shared]
            pbuf[q, rows_of(k), :] = jnp.concatenate(pieces, axis=0).astype(BF16)
            return carry

        lax.fori_loop(0, nx, step, 0)
        if k == 0:
            send(dn_hbm, dn.at[gu_rows], part_s.at[3], part_r.at[3], partner)
            send(sdn_hbm, sdn.at[gu_rows], part_s.at[4], part_r.at[4], partner)
        if DIRECT_SUM[k]:
            for d in range(1, nx):
                slot = k * (nx - 1) + d - 1
                send(pbuf.at[ring(x + d, nx), span(k)], rdir.at[d - 1, span(k)], dir_s.at[slot], dir_r.at[slot], x_peer(d))
        else:
            sum_send(k, 0, hmaj, 1, rmaj, maj_s, maj_r)
            sum_send(k, 0, hmin, -1, rmin, min_s, min_r)

    def sum_send(k, h, hops, way, recv, s, r):
        if h < hops:
            slot = k * hops + h
            view = pbuf.at[to_x(way * (hops - h)), span(k)]
            send(view, recv.at[h, span(k)], s.at[slot], r.at[slot], x_peer(sgn * way))

    def sum_hop(k, h, hops, way, recv, s, r):
        if h < hops:
            slot = k * hops + h
            arrived(recv.at[h - 1, span(k)], s.at[slot - 1], r.at[slot - 1])
            q = to_x(way * (hops - h))
            value = pbuf[q, rows_of(k), :].astype(F32) + recv[h - 1, rows_of(k), :].astype(F32)
            pbuf[q, rows_of(k), :] = value.astype(BF16)
            sum_send(k, h, hops, way, recv, s, r)

    def sum_hops(k, h):
        sum_hop(k, h, hmaj, 1, rmaj, maj_s, maj_r)
        sum_hop(k, h, hmin, -1, rmin, min_s, min_r)

    def activate(k):
        total = pbuf[x, rows_of(k), :].astype(F32)
        if DIRECT_SUM[k]:
            for d in range(1, nx):
                slot = k * (nx - 1) + d - 1
                arrived(rdir.at[d - 1, span(k)], dir_s.at[slot], dir_r.at[slot])
                total = total + rdir[d - 1, rows_of(k), :].astype(F32)
        else:
            for hops, recv, s, r in ((hmaj, rmaj, maj_s, maj_r), (hmin, rmin, min_s, min_r)):
                if hops:
                    slot = k * hops + hops - 1
                    arrived(recv.at[hops - 1, span(k)], s.at[slot], r.at[slot])
                    total = total + recv[hops - 1, rows_of(k), :].astype(F32)
        wide = unit_cols // 2
        left, right = total[:, :wide], total[:, wide:]
        low = lax.broadcasted_iota(jnp.int32, left.shape, 1) < wide // 2
        gate = jnp.where(low, left, pltpu.roll(right, wide // 2, 1))
        upper = jnp.where(low, pltpu.roll(left, wide // 2, 1), right)
        hid[x, rows_of(k), :] = (gate / (1.0 + jnp.exp(-gate)) * upper).astype(BF16)
        if DIRECT_GATHER[k]:
            view = hid.at[x, span(k)]
            for d in range(1, nx):
                slot = k * (nx - 1) + d - 1
                send(view, view, gdir_s.at[slot], gdir_r.at[slot], x_peer(d))
        else:
            gather_hop(k, 1, hmaj, 1, gmaj_s, gmaj_r)
            gather_hop(k, 1, hmin, -1, gmin_s, gmin_r)

    def gather_hop(k, h, hops, way, s, r):
        if h <= hops:
            view = hid.at[to_x(-way * (h - 1)), span(k)]
            slot = k * hops + h - 1
            send(view, view, s.at[slot], r.at[slot], x_peer(sgn * way))

    def gather_wait(k, h, hops, way, s, r):
        if h <= hops:
            slot = k * hops + h - 1
            arrived(hid.at[to_x(-way * h), span(k)], s.at[slot], r.at[slot])

    def gather_hops(k, h):
        gather_wait(k, h, hmaj, 1, gmaj_s, gmaj_r)
        gather_hop(k, h + 1, hmaj, 1, gmaj_s, gmaj_r)
        gather_wait(k, h, hmin, -1, gmin_s, gmin_r)
        gather_hop(k, h + 1, hmin, -1, gmin_s, gmin_r)

    def finish_chunk(k):
        if DIRECT_GATHER[k]:
            for d in range(1, nx):
                slot = k * (nx - 1) + d - 1
                arrived(hid.at[ring(x - d, nx), span(k)], gdir_s.at[slot], gdir_r.at[slot])
        else:
            gather_hops(k, hmaj)
        if k == 0:
            own[2].wait()
            arrived(dn.at[other_rows], part_s.at[3], part_r.at[3])
        hidden = jnp.concatenate([hid[q, rows_of(k), :] for q in range(nx)], axis=1)
        result = dot_rows(hidden, dn[...]).astype(BF16)
        for i in range(sizes[k]):
            b = first_block[k] + i
            block = result[i * rows : (i + 1) * rows]
            if b == 0:
                rbuf[0:rows, :] = block
            else:
                obuf[b * rows : (b + 1) * rows, :] = block
                send(obuf.at[one(b)], rbuf.at[one(b)], ret_s.at[b - 1], ret_r.at[b - 1], second_peer(-offsets[b]))
        for i in range(sizes[k]):
            number = first_block[k] + i - first_shared
            if number >= 0:
                top = (i + 1) * rows - 16
                hs[number * 8 : (number + 1) * 8, :] = hidden[top : top + 16].astype(F32)[8:16]

    def place(g, index):
        node_index, which = jnp.zeros_like(index), jnp.zeros_like(index)
        for i in range(1, side):
            node_index = node_index + jnp.where(index >= i * lengths[g], 1, 0)
        number = index - node_index * lengths[g]
        for i in range(1, groups[g][3]):
            which = which + jnp.where(number >= i * half, 1, 0)
        return node_index, number < groups[g][3] * half, which, number - which * half

    def forward_span(g):
        return pl.ds(first_row[g], lengths[g])

    def forward_group(g):
        _, _, block, size = groups[g]
        for b in range(block, block + size):
            if b > 0:
                arrived(rbuf.at[one(b)], ret_s.at[b - 1], ret_r.at[b - 1])
        length = lengths[g]
        shape = (side * length, size * rows)
        node_index, used, which, slot = place(g, lax.broadcasted_iota(jnp.int32, (shape[0], 1), 0))
        source = jnp.where(used, which * rows + slot * side + node_index, -1)
        moved = jnp.where(lax.broadcasted_iota(jnp.int32, shape, 1) == source, 1.0, 0.0).astype(BF16)
        result = dot(moved, rbuf[block * rows : (block + size) * rows, :]).astype(BF16)
        for i in range(side):
            fwd[i, first_row[g] : first_row[g] + length, :] = result[i * length : (i + 1) * length]
        for d in range(1, side):
            slot = g * (side - 1) + d - 1
            send(
                fwd.at[ring(a1 + d, side), forward_span(g)], frow.at[a1, forward_span(g)],
                fwd_s.at[slot], fwd_r.at[slot], first_peer(d),
            )
        frow[a1, first_row[g] : first_row[g] + length, :] = fwd[a1, first_row[g] : first_row[g] + length, :]

    def weigh_group(g):
        _, _, block, size = groups[g]
        length = lengths[g]
        node_index, used, which, slot = place(g, lax.broadcasted_iota(jnp.int32, (1, side * length), 1))
        shift = jnp.zeros_like(which)
        for i in range(size):
            shift = jnp.where(which == i, offsets[block + i], shift)
        second = (a2 + shift + side) & (side - 1)
        m = node_index * stride1 + second * stride2
        want = (m >> (experts.bit_length() - 1)) * 32 + slot + half * c
        want = jnp.where(used, want, -5).astype(F32)
        chosen_expert = lax.broadcasted_iota(jnp.int32, (experts, side * length), 0) == (m & (experts - 1))
        chosen_expert = jnp.where(chosen_expert, 1.0, 0.0).astype(BF16)
        ends = (((0,), (0,)), ((), ()))
        found = lax.dot_general(meta[a1].astype(BF16), chosen_expert, ends, preferred_element_type=F32)
        weight = lax.dot_general(gates[...].astype(BF16), chosen_expert, ends, preferred_element_type=F32)
        comb[:, first_row[g] * side : (first_row[g] + length) * side] = jnp.where(found == want, weight, 0.0).astype(BF16)

    def add_group(g):
        length = lengths[g]
        for d in range(1, side):
            slot = g * (side - 1) + d - 1
            arrived(frow.at[ring(a1 - d, side), forward_span(g)], fwd_s.at[slot], fwd_r.at[slot])
        landed = frow[:, first_row[g] : first_row[g] + length, :].reshape(side * length, 2 * width)
        acc[...] += dot(comb[:, first_row[g] * side : (first_row[g] + length) * side], landed)

    def shared_finish():
        own[3].wait()
        arrived(sdn.at[other_rows], part_s.at[4], part_r.at[4])
        mine_rows = pl.ds(pl.multiple_of(c * th, 8), th)
        acc[mine_rows, :] += dot_rows(hs[...].astype(BF16), sdn[...])

    schedule = []
    for k in range(chunks):
        steps = [start_chunk]
        if not DIRECT_SUM[k]:
            steps += [functools.partial(lambda h, k: sum_hops(k, h), h) for h in range(1, hmaj)]
        steps += [activate]
        if not DIRECT_GATHER[k]:
            steps += [functools.partial(lambda h, k: gather_hops(k, h), h) for h in range(1, hmaj)]
        steps += [finish_chunk]
        for i, f in enumerate(steps):
            schedule.append((STARTS[k] + i, k, f))
        finish = STARTS[k] + len(steps) - 1
        for g, group in enumerate(groups):
            if group[1] == k:
                schedule.append((STARTS[0] + 2 + g, chunks, functools.partial(lambda g, _: weigh_group(g), g)))
                schedule.append((finish + FORWARD_LAG, k, functools.partial(lambda g, _: forward_group(g), g)))
                schedule.append((finish + ADD_LAG, k, functools.partial(lambda g, _: add_group(g), g)))
    schedule.sort(key=lambda item: item[:2])
    acc[...] = jnp.zeros_like(acc)
    for _, k, f in schedule:
        f(k)
        if f is finish_chunk and k == chunks - 1:
            shared_finish()
    total = acc[...]
    low, high = total[:, :width], total[:, width:]
    first = c == 0
    fsend[...] = jnp.where(first, high, low)
    send(fsend, frecv, part_s.at[5], part_r.at[5], partner)
    keep = jnp.where(first, low, high)
    arrived(frecv, part_s.at[5], part_r.at[5])
    out_ref[...] = (keep + frecv[...]).astype(BF16)
    for copy in pending:
        copy.wait_send()


def build(mesh, most):
    nodes, locals_ = mesh.shape["node"], mesh.shape["local"]
    side, nx = math.isqrt(nodes), locals_ // 2

    def shards(tokens, expert_ids, route_weight, pool_offset, gate_up, down_proj, shared_gate_up, shared_down):
        tn, width = tokens.shape
        experts = pool_offset.shape[1]
        pools = nodes // experts
        half = most // pools // 2
        rows = half * side + 8
        sizes = CHUNKS[side]
        chunks = len(sizes)
        forwarded = sum(forward_rows(group[3], half) for group in groups_of(side))
        parcels = len(GROUPS[side]) * (side - 1)
        two = shared_gate_up.shape[1]
        ff = two // 2
        cols = two // nx
        every = side * rows
        hmaj, hmin = nx // 2, max(nx - 1 - nx // 2, 1)
        cfg = dict(side=side, nx=nx, experts=experts, pools=pools, half=half, rows=rows)
        long_way = side // 2
        dma = pltpu.SemaphoreType.DMA
        scratch = [
            pltpu.VMEM((2 * width, two), BF16),
            pltpu.VMEM((2 * width, two), BF16),
            pltpu.VMEM((2 * width, ff), BF16),
            pltpu.VMEM((2 * width, ff), BF16),
            pltpu.VMEM((2, tn, width), BF16),
            pltpu.VMEM((side, tn, 2 * width), BF16),
            pltpu.VMEM((side, experts, tn), F32),
            pltpu.VMEM((experts, tn), F32),
            pltpu.VMEM((experts, side * tn), F32),
            pltpu.VMEM((every, side * tn), BF16),
            pltpu.VMEM((every, 2 * width), BF16),
            pltpu.VMEM((every, 2 * width), BF16),
            pltpu.VMEM((nx, tn // 2, cols), F32),
            pltpu.VMEM((nx, every, cols), BF16),
            pltpu.VMEM((hmaj, every, cols), BF16),
            pltpu.VMEM((hmin, every, cols), BF16),
            pltpu.VMEM((nx - 1, every, cols), BF16),
            pltpu.VMEM((nx, every, cols // 2), BF16),
            pltpu.VMEM((tn // 2, ff), F32),
            pltpu.VMEM((every, 2 * width), BF16),
            pltpu.VMEM((every, 2 * width), BF16),
            pltpu.VMEM((side, forwarded, 2 * width), BF16),
            pltpu.VMEM((side, forwarded, 2 * width), BF16),
            pltpu.VMEM((tn, side * forwarded), BF16),
            pltpu.VMEM((tn, 2 * width), F32),
            pltpu.VMEM((tn, width), F32),
            pltpu.VMEM((tn, width), F32),
            dma((6,)), dma((6,)), dma((4,)),
            dma((2 * PIECES * long_way,)), dma((2 * PIECES * long_way,)),
            dma((side - 1,)), dma((side - 1,)),
            dma((side - 1,)), dma((side - 1,)),
            dma((chunks * hmaj,)), dma((chunks * hmaj,)),
            dma((chunks * hmin,)), dma((chunks * hmin,)),
            dma((chunks * (nx - 1),)), dma((chunks * (nx - 1),)),
            dma((chunks * hmaj,)), dma((chunks * hmaj,)),
            dma((chunks * hmin,)), dma((chunks * hmin,)),
            dma((chunks * (nx - 1),)), dma((chunks * (nx - 1),)),
            dma((side - 1,)), dma((side - 1,)),
            dma((parcels,)), dma((parcels,)),
        ]
        vmem, hbm = pl.BlockSpec(memory_space=pltpu.VMEM), pl.BlockSpec(memory_space=pl.ANY)
        return pl.pallas_call(
            functools.partial(kernel, cfg),
            out_shape=jax.ShapeDtypeStruct((tn, width), BF16),
            in_specs=[vmem] * 4 + [hbm] * 4,
            out_specs=vmem,
            scratch_shapes=scratch,
            compiler_params=pltpu.CompilerParams(
                collective_id=0, has_side_effects=True, vmem_limit_bytes=56 * 1024 * 1024
            ),
        )(
            expert_ids.T, route_weight.T, pool_offset, tokens,
            gate_up[0], down_proj[0].T, shared_gate_up, shared_down.T,
        )

    placed = (
        P("node", "local"),
        P("node", None),
        P("node", None),
        P("node", None),
        P("node", "local", None),
        P("node", None, "local"),
        P("local", None),
        P(None, "local"),
    )
    return jax.shard_map(
        shards, mesh=mesh, in_specs=placed, out_specs=P("node", "local"), check_vma=False
    )


def solution(mesh):
    return build(mesh, MOST)
```
